32 devices in a mesh: ctx: 8 (over y, x, core), tp: 4 (over z).
Axes of the slice: x: 2, y: 2, z: 4, core: 2. Of those that a mesh axis runs over, the one named last changes fastest.
Arguments:
- queries: bfloat16 [1024, 128, 128], P('ctx', 'tp'), may hold values from -8 to 8
- fresh_rotated_keys: bfloat16 [1024, 8, 128], P('ctx', 'tp'), may hold values from -4 to 4
- fresh_value_rows: bfloat16 [1024, 8, 128], P('ctx', 'tp'), may hold values from -5 to 5
- cache_keys: bfloat16 [8192, 8, 128], P('ctx', 'tp'), may hold values from -4 to 4
- prefix_value_rows: bfloat16 [8192, 8, 128], P('ctx', 'tp'), may hold values from -5 to 5
- cache_lengths: int32 [8], P('ctx'), may hold values from 256 to 1024, as said below
- new_segment: int32 [1024], replicated, may hold values from 0 to 3, never falling along the last dimension, each value on 1 to 512 neighbouring positions
- out_weight: bfloat16 [16384, 16384], P('tp', 'ctx'), may hold values from -0.1875 to 0.1875
Outputs:
- attended: bfloat16 [1024, 128, 128], P('ctx', 'tp')
- mixed: bfloat16 [1024, 16384], P('tp', 'ctx')
The draws below stay inside these ranges and needn't reach their ends.
Inputs may be any that keep to these rules, and one draw needn't show every extreme that they name: `cache_lengths`: slots at or after the length of their index are unused; some index is full in every draw.
All inputs are finite; a program needn't handle non-finite values.
Results may differ from the reference program's by a relative error of at most 0.015.
Values may be sent and summed in bfloat16 or wider, within the bound.
A program may use at most 128 MiB of HBM per device.

```python
import math
import jax
import jax.numpy as jnp
import numpy as np
from jax import lax

QUERY_HEADS = 128
KEY_VALUE_HEADS = 8
HEAD_SIZE = 128
D = 16384
QUERY_DEV = 128
CACHE_DEV = 1024
SEGS = 4
NEW_TOKEN_TOTAL = 1024
CACHE_SLOT_TOTAL = 8192
N_CTX = 8


def draw_queries(key, part):
    base_offset = jnp.clip(2.5 * jax.random.normal(jax.random.fold_in(key, 1), (NEW_TOKEN_TOTAL, QUERY_HEADS, HEAD_SIZE), jnp.float32), -8.0, 8.0)
    return base_offset.astype(jnp.bfloat16)


def draw_cache_keys(key, part):
    base_offset = jnp.clip(jax.random.normal(jax.random.fold_in(key, 5), (CACHE_SLOT_TOTAL, KEY_VALUE_HEADS, HEAD_SIZE), jnp.float32), -4.0, 4.0)
    return base_offset.astype(jnp.bfloat16)


def draw_cache_lengths(key, part):
    count = CACHE_SLOT_TOTAL // CACHE_DEV
    lengths = jax.random.randint(jax.random.fold_in(key, 2), (count,), CACHE_DEV // 4, CACHE_DEV + 1)
    picked = jax.random.randint(jax.random.fold_in(key, 3), (), 0, count)
    return lengths.at[picked].set(CACHE_DEV).astype(jnp.int32)


def shard_levels(own_key, extent, shards, smallest, top_value):
    factor_of = 1.0
    for position, shards_of in shards:
        draws = jax.random.uniform(jax.random.fold_in(jax.random.fold_in(own_key, 6), position), (shards_of,), jnp.float32, smallest / len(shards), top_value / len(shards))
        factor_of = factor_of * jnp.repeat(jnp.exp(draws), extent[position] // shards_of).reshape((-1,) + (1,) * (len(extent) - 1 - position))
    return factor_of


def split_up(amount, total, most, lean):
    portions = [(1 << 20) // math.isqrt(grade ** lean) + 1 for grade in range(2, amount + 1)]
    rest, holding = total - most - (amount - 1), [1] * (amount - 1)
    while rest > 0:
        candidates = [i for i in range(amount - 1) if holding[i] < most]
        mass, left = sum([portions[i] for i in candidates]), rest
        for i in candidates:
            more = min(most - holding[i], max(1, left * portions[i] // mass), rest)
            holding[i] = holding[i] + more
            rest = rest - more
    return np.array([most] + holding)


def ragged(own_key, count, total, most, lean):
    if count == 2:
        one = jax.random.randint(own_key, (), max(1, total - most), min(most, total - 1) + 1)
        return jnp.stack([one, total - one])
    sizes = jnp.asarray(split_up(count, total, most, lean), jnp.int32)
    pairs = (count - 1) // 2
    donor, receiver = sizes[1:1 + 2 * pairs:2], sizes[2:2 + 2 * pairs:2]
    room = jnp.minimum(donor - 1, most - receiver)
    moved = jax.random.randint(jax.random.fold_in(own_key, 1), (pairs,), 0, 1 << 20) % (room + 1)
    sizes = sizes.at[1:1 + 2 * pairs:2].set(donor - moved).at[2:2 + 2 * pairs:2].set(receiver + moved)
    return sizes[jax.random.permutation(jax.random.fold_in(own_key, 2), count)]


def scatter_about(rng, shape, deviation, limit, split=(), kind=jnp.bfloat16):
    factor_of = shard_levels(rng, shape, split, -0.22, 0.18) if split else 1.0
    entries = jax.random.normal(rng, shape, jnp.float32) * deviation * factor_of
    return jnp.minimum(jnp.maximum(entries, -limit), limit).astype(kind)


def setup_inputs(seed: int = 0) -> dict:
    key_of = jax.random.split(jax.random.key(seed), 9)
    return {
        "queries": draw_queries(jax.random.fold_in(key_of[8], 71), 0),
        "fresh_rotated_keys": scatter_about(key_of[1], (NEW_TOKEN_TOTAL, KEY_VALUE_HEADS, HEAD_SIZE), 1.0, 4.0, ((0, 8), (1, 4))),
        "fresh_value_rows": scatter_about(key_of[2], (NEW_TOKEN_TOTAL, KEY_VALUE_HEADS, HEAD_SIZE), 1.0, 5.0, ((0, 8), (1, 4))),
        "cache_keys": draw_cache_keys(jax.random.fold_in(key_of[8], 71), 0),
        "prefix_value_rows": scatter_about(key_of[4], (CACHE_SLOT_TOTAL, KEY_VALUE_HEADS, HEAD_SIZE), 1.0, 5.0, ((0, 8), (1, 4))),
        "cache_lengths": draw_cache_lengths(jax.random.fold_in(key_of[8], 71), 0),
        "new_segment": jnp.searchsorted(jnp.cumsum(ragged(key_of[6], SEGS, NEW_TOKEN_TOTAL, NEW_TOKEN_TOTAL // 2, 2)), jnp.arange(NEW_TOKEN_TOTAL), side="right").astype(jnp.int32),
        "out_weight": scatter_about(key_of[7], (QUERY_HEADS * HEAD_SIZE, D), (QUERY_HEADS * HEAD_SIZE // 16) ** -0.5, 0.1875, ((0, 4), (1, 8))),
    }


lowest_score_bound = -1e30


def attend(query_head, key_rows, value_rows, visible, scaling):
    scores = jnp.einsum("qrd,kd->qrk", query_head, key_rows) * scaling
    scores = jnp.where(visible[:, None, :], scores, lowest_score_bound)
    highest = jnp.max(scores, axis=-1)
    weights = jnp.exp(scores - highest[..., None])
    total = jnp.sum(weights, axis=-1)
    rounded = lax.optimization_barrier(weights.astype(jnp.bfloat16)).astype(jnp.float32)
    mixture = jnp.einsum("qrk,kd->qrd", rounded, value_rows) / total[..., None]
    return mixture.astype(jnp.bfloat16), highest + jnp.log(total)


def reference(queries, fresh_rotated_keys, fresh_value_rows, cache_keys, prefix_value_rows, cache_lengths, new_segment, out_weight):
    query_group = QUERY_HEADS // KEY_VALUE_HEADS
    scaling = HEAD_SIZE ** -0.5
    every_query_row = jnp.moveaxis(queries.astype(jnp.float32).reshape(NEW_TOKEN_TOTAL, KEY_VALUE_HEADS, query_group, HEAD_SIZE), 1, 0)
    positions = jnp.arange(NEW_TOKEN_TOTAL, dtype=jnp.int32)
    slots = jnp.arange(CACHE_DEV, dtype=jnp.int32)

    def shard_step(state, shard):
        run_max, run_sum, accum = state
        start_cache = (shard * CACHE_DEV).astype(jnp.int32)
        start_new = (shard * QUERY_DEV).astype(jnp.int32)
        key_rows = jnp.concatenate([lax.dynamic_slice_in_dim(cache_keys, start_cache, CACHE_DEV, 0), lax.dynamic_slice_in_dim(fresh_rotated_keys, start_new, QUERY_DEV, 0)], 0).astype(jnp.float32)
        value_rows = jnp.concatenate([lax.dynamic_slice_in_dim(prefix_value_rows, start_cache, CACHE_DEV, 0), lax.dynamic_slice_in_dim(fresh_value_rows, start_new, QUERY_DEV, 0)], 0).astype(jnp.float32)
        length = lax.dynamic_slice_in_dim(cache_lengths, shard, 1, 0)[0]
        key_pos = start_new + jnp.arange(QUERY_DEV, dtype=jnp.int32)
        key_seg = lax.dynamic_slice_in_dim(new_segment, start_new, QUERY_DEV, 0)
        cache_ok = jnp.broadcast_to((slots < length)[None, :], (NEW_TOKEN_TOTAL, CACHE_DEV))
        new_ok = (new_segment[:, None] == key_seg[None, :]) & (key_pos[None, :] <= positions[:, None])
        visible = jnp.concatenate([cache_ok, new_ok], 1)

        def per_head(inputs):
            query_head, key_head, value_head = inputs
            return attend(query_head, key_head, value_head, visible, scaling)

        mixtures, log_mass = lax.map(per_head, (every_query_row, jnp.moveaxis(key_rows, 1, 0), jnp.moveaxis(value_rows, 1, 0)))
        highest = jnp.maximum(run_max, log_mass)
        kept = jnp.exp(run_max - highest)
        fresh = jnp.exp(log_mass - highest)
        run_sum = run_sum * kept + fresh
        accum = accum * kept[..., None] + fresh[..., None] * mixtures.astype(jnp.float32)
        return (highest, run_sum, accum), None

    initial_state = (jnp.full((KEY_VALUE_HEADS, NEW_TOKEN_TOTAL, query_group), lowest_score_bound, jnp.float32), jnp.zeros((KEY_VALUE_HEADS, NEW_TOKEN_TOTAL, query_group), jnp.float32), jnp.zeros((KEY_VALUE_HEADS, NEW_TOKEN_TOTAL, query_group, HEAD_SIZE), jnp.float32))
    (run_max, run_sum, accum), _ = lax.scan(shard_step, initial_state, jnp.arange(N_CTX, dtype=jnp.int32))
    merged = accum / run_sum[..., None]
    attended = jnp.moveaxis(merged, 0, 1).reshape(NEW_TOKEN_TOTAL, QUERY_HEADS, HEAD_SIZE).astype(jnp.bfloat16)
    mixed = jnp.dot(attended.reshape(NEW_TOKEN_TOTAL, QUERY_HEADS * HEAD_SIZE), out_weight, preferred_element_type=jnp.float32).astype(jnp.bfloat16)
    return attended, mixed
```

```python
import functools
import math

import jax
import jax.numpy as jnp
from jax import lax
from jax.experimental import pallas as pl
from jax.experimental.pallas import tpu as pltpu
from jax.sharding import PartitionSpec as P

LOWEST = -1e30
KEY_BLOCK = 256
TOKEN_BLOCK = 32
CHUNKS = 2


def attention_kernel(
    counts_ref, bounds_ref, q_ref, lo_ref, k_ref, v_ref, o_ref, m_ref, acc_ref,
    *, sets, cache_rows, fresh_rows, head_rows, multiplier, first_token
):
    block = pl.program_id(1)
    tokens, group, width = q_ref.shape
    rows = tokens * group
    query = q_ref[...].reshape(rows, width)
    m_ref[...] = jnp.full(m_ref.shape, LOWEST, jnp.float32)
    acc_ref[...] = jnp.zeros(acc_ref.shape, jnp.float32)

    def update(scores, values):
        scores_max = jnp.max(scores, axis=0, keepdims=True) * multiplier
        old = m_ref[...]
        new = jnp.maximum(old, scores_max)
        m_ref[...] = new
        weights = jnp.exp2(scores * multiplier - new).astype(jnp.bfloat16)
        acc_ref[...] = acc_ref[...] * jnp.exp2(old - new) + jnp.dot(
            values, weights, preferred_element_type=jnp.float32
        )

    def score(keys):
        return lax.dot_general(
            keys, query, (((1,), (1,)), ((), ())), preferred_element_type=jnp.float32
        )

    def one_set(s, carry):
        def one_block(b, inner):
            start = pl.multiple_of(b * KEY_BLOCK, KEY_BLOCK)
            keys = k_ref[s, pl.ds(start, KEY_BLOCK), :]
            values = v_ref[s, :, pl.ds(start, KEY_BLOCK)]
            update(score(keys), values)
            return inner

        return lax.fori_loop(0, counts_ref[s], one_block, carry)

    lax.fori_loop(0, sets, one_set, 0)

    low = lo_ref[0:1, :]
    high = lo_ref[1:2, :]

    def one_fresh(s, carry):
        scores = score(k_ref[s, cache_rows : cache_rows + fresh_rows, :])
        position = s * fresh_rows + lax.broadcasted_iota(jnp.int32, scores.shape, 0)
        scores = jnp.where((position >= low) & (position <= high), scores, LOWEST)
        update(scores, v_ref[s, :, cache_rows : cache_rows + fresh_rows])
        return carry

    lax.fori_loop(bounds_ref[2 * block], bounds_ref[2 * block + 1], one_fresh, 0)
    total = acc_ref[width : width + 1, :]
    out = (acc_ref[0:width, :] / total).T
    o_ref[...] = out.astype(o_ref.dtype).reshape(tokens, group, width)


def attention(queries, first, tokens, key_sets, value_sets, counts, low, position):
    rows, heads, width = queries.shape
    sets, piece, _ = key_sets.shape
    kv_heads = key_sets.shape[2] // width
    value_rows = value_sets.shape[1] // kv_heads
    group = heads // kv_heads
    cache_rows = piece - rows
    blocks = tokens // TOKEN_BLOCK
    lanes = TOKEN_BLOCK * group
    chunk_low = low[first : first + tokens]
    chunk_position = position[first : first + tokens]
    pair = jnp.stack([chunk_low, chunk_position])
    pair = jnp.repeat(pair, group, axis=1)
    begin = chunk_low[::TOKEN_BLOCK] // rows
    end = chunk_position[TOKEN_BLOCK - 1 :: TOKEN_BLOCK] // rows + 1
    bounds = jnp.stack([begin, end], 1).reshape(-1)
    skip = first // TOKEN_BLOCK
    kernel = functools.partial(
        attention_kernel,
        sets=sets,
        cache_rows=cache_rows,
        fresh_rows=rows,
        head_rows=value_rows,
        multiplier=width**-0.5 * math.log2(math.e),
        first_token=first,
    )
    total_keys = sets * piece
    return pl.pallas_call(
        kernel,
        out_shape=jax.ShapeDtypeStruct((tokens, heads, width), jnp.bfloat16),
        grid_spec=pltpu.PrefetchScalarGridSpec(
            num_scalar_prefetch=2,
            grid=(kv_heads, blocks),
            in_specs=[
                pl.BlockSpec((TOKEN_BLOCK, group, width), lambda h, i, *_: (i + skip, h, 0)),
                pl.BlockSpec((2, lanes), lambda h, i, *_: (0, i)),
                pl.BlockSpec((sets, piece, width), lambda h, i, *_: (0, 0, h)),
                pl.BlockSpec((sets, value_rows, piece), lambda h, i, *_: (0, h, 0)),
            ],
            out_specs=pl.BlockSpec((TOKEN_BLOCK, group, width), lambda h, i, *_: (i, h, 0)),
            scratch_shapes=[
                pltpu.VMEM((1, lanes), jnp.float32),
                pltpu.VMEM((value_rows, lanes), jnp.float32),
            ],
        ),
        compiler_params=pltpu.CompilerParams(vmem_limit_bytes=48 * 1024 * 1024),
        cost_estimate=pl.CostEstimate(
            flops=4 * tokens * heads * width * total_keys,
            bytes_accessed=4 * total_keys * kv_heads * width,
            transcendentals=tokens * heads * total_keys,
        ),
    )(counts, bounds, queries, pair, key_sets, value_sets)


def pack(keys, fresh_keys, values, fresh_values, length):
    cache_rows, kv_heads, width = keys.shape
    fresh_rows = fresh_keys.shape[0]
    filled = jnp.arange(cache_rows, dtype=jnp.int32) < length
    flat_keys = keys.reshape(cache_rows, kv_heads * width)
    flat_keys = jnp.where(filled[:, None], flat_keys, flat_keys[0:1, :])
    flat_keys = jnp.concatenate([flat_keys, fresh_keys.reshape(fresh_rows, kv_heads * width)], 0)
    kept = jnp.where(filled[:, None, None], values, jnp.zeros_like(values))
    wide = jnp.concatenate([kept, fresh_values], 0).transpose(1, 2, 0)
    mask = jnp.concatenate([filled, jnp.ones((fresh_rows,), jnp.bool_)]).astype(jnp.bfloat16)
    mask = jnp.broadcast_to(mask[None, None, :], (kv_heads, 16, cache_rows + fresh_rows))
    wide = jnp.concatenate([wide, mask], 1).reshape(kv_heads * (width + 16), -1)
    return flat_keys, wide


def on_device(
    queries,
    fresh_rotated_keys,
    fresh_value_rows,
    cache_keys,
    prefix_value_rows,
    cache_lengths,
    new_segment,
    out_weight,
    *,
    ctx,
    tp,
):
    rows, heads, width = queries.shape
    kv_heads = fresh_rotated_keys.shape[1]
    cache_rows = cache_keys.shape[0]
    here = lax.axis_index("ctx")
    flat_keys, wide = pack(
        cache_keys, fresh_rotated_keys, prefix_value_rows, fresh_value_rows, cache_lengths[0]
    )
    key_sets = lax.all_gather(flat_keys, "ctx", axis=0)
    value_sets = lax.all_gather(wide, "ctx", axis=0)
    lengths = jnp.sum(value_sets[:, width, :cache_rows].astype(jnp.float32), axis=1)
    counts = (lengths.astype(jnp.int32) + KEY_BLOCK - 1) // KEY_BLOCK
    own_segment = lax.dynamic_slice_in_dim(new_segment, here * rows, rows, 0)
    low = jnp.sum((new_segment[None, :] < own_segment[:, None]).astype(jnp.int32), axis=1)
    position = here * rows + jnp.arange(rows, dtype=jnp.int32)

    step = rows // CHUNKS
    attended, mixed = [], []
    for c in range(CHUNKS):
        part = attention(
            queries, c * step, step, key_sets, value_sets, counts, low, position
        )
        attended.append(part)
        everyone = lax.all_gather(part.reshape(step, heads * width), "ctx", axis=0, tiled=True)
        sums = jnp.dot(everyone, out_weight, preferred_element_type=jnp.float32)
        sums = lax.psum_scatter(
            sums.astype(jnp.bfloat16), "tp", scatter_dimension=0, tiled=True
        )
        mixed.append(sums.reshape(ctx // tp, step, -1))
    attended = jnp.concatenate(attended, 0)
    mixed = jnp.stack(mixed, 1).reshape(ctx // tp * rows, -1)
    return attended, mixed


def solution(mesh):
    in_specs = (
        P("ctx", "tp", None),
        P("ctx", "tp", None),
        P("ctx", "tp", None),
        P("ctx", "tp", None),
        P("ctx", "tp", None),
        P("ctx"),
        P(),
        P("tp", "ctx"),
    )
    out_specs = (P("ctx", "tp", None), P("tp", "ctx"))
    return jax.shard_map(
        functools.partial(on_device, ctx=mesh.shape["ctx"], tp=mesh.shape["tp"]),
        mesh=mesh,
        in_specs=in_specs,
        out_specs=out_specs,
        check_vma=False,
    )
```

```python
import functools
import math

import jax
import jax.numpy as jnp
from jax import lax
from jax.experimental import pallas as pl
from jax.experimental.pallas import tpu as pltpu
from jax.sharding import PartitionSpec as P

LOWEST = -1e30
KEY_BLOCK = 256
TOKEN_BLOCK = 64
LANES = 256
CHUNKS = 2


def attention_kernel(
    counts_ref, bounds_ref, q_ref, lo_ref, k_ref, v_ref, o_ref, m_ref, acc_ref,
    *, sets, cache_rows, fresh_rows, multiplier
):
    block = pl.program_id(1)
    tokens, group, width = q_ref.shape
    rows = tokens * group
    m_ref[...] = jnp.full(m_ref.shape, LOWEST, jnp.float32)
    acc_ref[...] = jnp.zeros(acc_ref.shape, jnp.float32)
    part_tokens = LANES // group
    parts = [(pl.ds(p * LANES, LANES), p * part_tokens) for p in range(rows // LANES)]

    def update(all_scores, values):
        olds = [m_ref[:, lanes] for lanes, _ in parts]
        news = [
            jnp.maximum(old, jnp.max(scores, axis=0, keepdims=True) * multiplier)
            for old, scores in zip(olds, all_scores)
        ]
        sums = []
        for scores, new in zip(all_scores, news):
            weights = jnp.exp2(scores * multiplier - new).astype(jnp.bfloat16)
            sums.append(jnp.dot(values, weights, preferred_element_type=jnp.float32))
        for (lanes, _), old, new, part in zip(parts, olds, news, sums):
            m_ref[:, lanes] = new
            acc_ref[:, lanes] = acc_ref[:, lanes] * jnp.exp2(old - new) + part

    def score(keys):
        return [
            lax.dot_general(
                keys,
                q_ref[start : start + part_tokens].reshape(LANES, width),
                (((1,), (1,)), ((), ())),
                preferred_element_type=jnp.float32,
            )
            for _, start in parts
        ]

    def one_set(s, carry):
        def one_block(b, inner):
            start = pl.multiple_of(b * KEY_BLOCK, KEY_BLOCK)
            keys = k_ref[s, pl.ds(start, KEY_BLOCK), :]
            values = v_ref[s, :, pl.ds(start, KEY_BLOCK)]
            update(score(keys), values)
            return inner

        return lax.fori_loop(0, counts_ref[s], one_block, carry)

    lax.fori_loop(0, sets, one_set, 0)

    def one_fresh(s, carry):
        all_scores = []
        first = s * fresh_rows
        scores = score(k_ref[s, cache_rows : cache_rows + fresh_rows, :])
        for (lanes, _), part in zip(parts, scores):
            place = first + lax.broadcasted_iota(jnp.int32, part.shape, 0)
            seen = (place >= lo_ref[0:1, lanes]) & (place <= lo_ref[1:2, lanes])
            all_scores.append(jnp.where(seen, part, LOWEST))
        update(all_scores, v_ref[s, :, cache_rows : cache_rows + fresh_rows])
        return carry

    lax.fori_loop(bounds_ref[2 * block], bounds_ref[2 * block + 1], one_fresh, 0)
    for lanes, start in parts:
        total = acc_ref[width : width + 1, lanes]
        out = (acc_ref[0:width, lanes] / total).T
        o_ref[start : start + part_tokens] = out.astype(o_ref.dtype).reshape(
            part_tokens, group, width
        )


def gather_kernel(a_ref, b_ref, a_out, b_out, local_sem, send_sem, recv_sem):
    me = lax.axis_index("ctx")
    column = lax.rem(me // 2, 2)
    line = me // 4
    along_x = me + 2 - 4 * column
    along_y = me + 4 - 8 * line
    across = along_y + 2 - 4 * column
    core = lax.rem(me, 2)
    other = me + 1 - 2 * core

    barrier = pltpu.get_barrier_semaphore()
    for partner in (along_x, along_y, other):
        pl.semaphore_signal(
            barrier, inc=1, device_id={"ctx": partner}, device_id_type=pl.DeviceIdType.MESH
        )
    pl.semaphore_wait(barrier, 3)

    def send(which, slot, source, owner, partner):
        out = (a_out, b_out)[which]
        copy = pltpu.make_async_remote_copy(
            src_ref=source,
            dst_ref=out.at[owner],
            send_sem=send_sem.at[which, slot],
            recv_sem=recv_sem.at[which, slot],
            device_id={"ctx": partner},
            device_id_type=pl.DeviceIdType.MESH,
        )
        copy.start()
        return copy

    copies = []
    keep = []
    for which, (source, out) in enumerate(((a_ref, a_out), (b_ref, b_out))):
        by_x = send(which, 0, source, me, along_x)
        by_y = send(which, 1, source, me, along_y)
        inside = send(which, 2, source, me, other)
        copies.append([by_x, by_y, inside])
        local = pltpu.make_async_copy(source, out.at[me], local_sem.at[which])
        local.start()
        keep.append(local)

    a_copies, b_copies = copies
    a_copies[0].wait_recv()
    a_copies.append(send(0, 3, a_out.at[along_x], along_x, along_y))
    a_copies.append(send(0, 4, a_out.at[along_x], along_x, other))
    b_copies[1].wait_recv()
    b_copies.append(send(1, 3, b_out.at[along_y], along_y, along_x))
    b_copies.append(send(1, 4, b_out.at[along_y], along_y, other))
    a_copies[1].wait_recv()
    a_copies.append(send(0, 5, a_out.at[along_y], along_y, other))
    b_copies[0].wait_recv()
    b_copies.append(send(1, 5, b_out.at[along_x], along_x, other))
    a_copies[3].wait_recv()
    a_copies.append(send(0, 6, a_out.at[across], across, other))
    b_copies[3].wait_recv()
    b_copies.append(send(1, 6, b_out.at[across], across, other))
    for group in copies:
        for slot in (2, 4, 5, 6):
            group[slot].wait_recv()
        for copy in group:
            copy.wait_send()
    for local in keep:
        local.wait()


def gather_pair(a, b, ctx, collective_id):
    if ctx != 8:
        return lax.all_gather(a, "ctx", axis=0), lax.all_gather(b, "ctx", axis=0)
    return pl.pallas_call(
        gather_kernel,
        out_shape=[jax.ShapeDtypeStruct((ctx,) + x.shape, x.dtype) for x in (a, b)],
        in_specs=[pl.BlockSpec(memory_space=pl.ANY)] * 2,
        out_specs=[pl.BlockSpec(memory_space=pl.ANY)] * 2,
        scratch_shapes=[
            pltpu.SemaphoreType.DMA((2,)),
            pltpu.SemaphoreType.DMA((2, 7)),
            pltpu.SemaphoreType.DMA((2, 7)),
        ],
        compiler_params=pltpu.CompilerParams(collective_id=collective_id, has_side_effects=True),
        cost_estimate=pl.CostEstimate(
            flops=0, bytes_accessed=16 * (a.size + b.size), transcendentals=0
        ),
    )(a, b)


def attention(queries, first, tokens, key_sets, value_sets, counts, low, position):
    rows, heads, width = queries.shape
    sets, piece, _ = key_sets.shape
    kv_heads = key_sets.shape[2] // width
    value_rows = value_sets.shape[1] // kv_heads
    group = heads // kv_heads
    cache_rows = piece - rows
    blocks = tokens // TOKEN_BLOCK
    lanes = TOKEN_BLOCK * group
    chunk_low = low[first : first + tokens]
    chunk_position = position[first : first + tokens]
    pair = jnp.stack([chunk_low, chunk_position])
    pair = jnp.repeat(pair, group, axis=1)
    begin = chunk_low[::TOKEN_BLOCK] // rows
    end = chunk_position[TOKEN_BLOCK - 1 :: TOKEN_BLOCK] // rows + 1
    bounds = jnp.stack([begin, end], 1).reshape(-1)
    skip = first // TOKEN_BLOCK
    kernel = functools.partial(
        attention_kernel,
        sets=sets,
        cache_rows=cache_rows,
        fresh_rows=rows,
        multiplier=width**-0.5 * math.log2(math.e),
    )
    total_keys = sets * piece
    return pl.pallas_call(
        kernel,
        out_shape=jax.ShapeDtypeStruct((tokens, heads, width), jnp.bfloat16),
        grid_spec=pltpu.PrefetchScalarGridSpec(
            num_scalar_prefetch=2,
            grid=(kv_heads, blocks),
            in_specs=[
                pl.BlockSpec((TOKEN_BLOCK, group, width), lambda h, i, *_: (i + skip, h, 0)),
                pl.BlockSpec((2, lanes), lambda h, i, *_: (0, i)),
                pl.BlockSpec((sets, piece, width), lambda h, i, *_: (0, 0, h)),
                pl.BlockSpec((sets, value_rows, piece), lambda h, i, *_: (0, h, 0)),
            ],
            out_specs=pl.BlockSpec((TOKEN_BLOCK, group, width), lambda h, i, *_: (i, h, 0)),
            scratch_shapes=[
                pltpu.VMEM((1, lanes), jnp.float32),
                pltpu.VMEM((value_rows, lanes), jnp.float32),
            ],
        ),
        compiler_params=pltpu.CompilerParams(vmem_limit_bytes=48 * 1024 * 1024),
        cost_estimate=pl.CostEstimate(
            flops=4 * tokens * heads * width * total_keys,
            bytes_accessed=4 * total_keys * kv_heads * width,
            transcendentals=tokens * heads * total_keys,
        ),
    )(counts, bounds, queries, pair, key_sets, value_sets)


def pack(keys, fresh_keys, values, fresh_values, length):
    cache_rows, kv_heads, width = keys.shape
    fresh_rows = fresh_keys.shape[0]
    filled = jnp.arange(cache_rows, dtype=jnp.int32) < length
    flat_keys = keys.reshape(cache_rows, kv_heads * width)
    flat_keys = jnp.where(filled[:, None], flat_keys, flat_keys[0:1, :])
    flat_keys = jnp.concatenate([flat_keys, fresh_keys.reshape(fresh_rows, kv_heads * width)], 0)
    kept = jnp.where(filled[:, None, None], values, jnp.zeros_like(values))
    wide = jnp.concatenate([kept, fresh_values], 0).transpose(1, 2, 0)
    mask = jnp.concatenate([filled, jnp.ones((fresh_rows,), jnp.bool_)]).astype(jnp.bfloat16)
    mask = jnp.broadcast_to(mask[None, None, :], (kv_heads, 16, cache_rows + fresh_rows))
    wide = jnp.concatenate([wide, mask], 1).reshape(kv_heads * (width + 16), -1)
    return flat_keys, wide


def on_device(
    queries,
    fresh_rotated_keys,
    fresh_value_rows,
    cache_keys,
    prefix_value_rows,
    cache_lengths,
    new_segment,
    out_weight,
    *,
    ctx,
    tp,
):
    rows, heads, width = queries.shape
    kv_heads = fresh_rotated_keys.shape[1]
    cache_rows = cache_keys.shape[0]
    here = lax.axis_index("ctx")
    flat_keys, wide = pack(
        cache_keys, fresh_rotated_keys, prefix_value_rows, fresh_value_rows, cache_lengths[0]
    )
    key_sets, value_sets = gather_pair(flat_keys, wide, ctx, 0)
    lengths = jnp.sum(value_sets[:, width, :cache_rows].astype(jnp.float32), axis=1)
    counts = (lengths.astype(jnp.int32) + KEY_BLOCK - 1) // KEY_BLOCK
    own_segment = lax.dynamic_slice_in_dim(new_segment, here * rows, rows, 0)
    low = jnp.sum((new_segment[None, :] < own_segment[:, None]).astype(jnp.int32), axis=1)
    position = here * rows + jnp.arange(rows, dtype=jnp.int32)

    step = rows // CHUNKS
    attended, mixed = [], []
    for c in range(CHUNKS):
        part = attention(
            queries, c * step, step, key_sets, value_sets, counts, low, position
        )
        attended.append(part)
        flat = part.reshape(step, heads * width)
        halves = gather_pair(flat[: step // 2], flat[step // 2 :], ctx, c + 1)
        everyone = jnp.concatenate(halves, 1).reshape(ctx * step, heads * width)
        if mixed:
            everyone, mixed[-1] = lax.optimization_barrier((everyone, mixed[-1]))
        sums = jnp.dot(everyone, out_weight, preferred_element_type=jnp.float32)
        sums = sums.astype(jnp.bfloat16)
        queries, sums = lax.optimization_barrier((queries, sums))
        sums = lax.psum_scatter(sums, "tp", scatter_dimension=0, tiled=True)
        mixed.append(sums.reshape(ctx // tp, step, -1))
    attended = jnp.concatenate(attended, 0)
    mixed = jnp.stack(mixed, 1).reshape(ctx // tp * rows, -1)
    return attended, mixed


def solution(mesh):
    in_specs = (
        P("ctx", "tp", None),
        P("ctx", "tp", None),
        P("ctx", "tp", None),
        P("ctx", "tp", None),
        P("ctx", "tp", None),
        P("ctx"),
        P(),
        P("tp", "ctx"),
    )
    out_specs = (P("ctx", "tp", None), P("tp", "ctx"))
    return jax.shard_map(
        functools.partial(on_device, ctx=mesh.shape["ctx"], tp=mesh.shape["tp"]),
        mesh=mesh,
        in_specs=in_specs,
        out_specs=out_specs,
        check_vma=False,
    )
```

```python
import functools
import math

import jax
import jax.numpy as jnp
from jax import lax
from jax.experimental import pallas as pl
from jax.experimental.pallas import tpu as pltpu
from jax.sharding import PartitionSpec as P

LOWEST = -1e30
KEY_BLOCK = 256
TOKEN_BLOCK = 64
LANES = 256
CHUNKS = 2


def attention_kernel(
    counts_ref, bounds_ref, q_ref, lo_ref, k_ref, v_ref, o_ref, m_ref, acc_ref,
    *, sets, cache_rows, fresh_rows, multiplier
):
    block = pl.program_id(1)
    tokens, group, width = q_ref.shape
    rows = tokens * group
    m_ref[...] = jnp.full(m_ref.shape, LOWEST, jnp.float32)
    acc_ref[...] = jnp.zeros(acc_ref.shape, jnp.float32)
    part_tokens = LANES // group
    parts = [(pl.ds(p * LANES, LANES), p * part_tokens) for p in range(rows // LANES)]

    def update(all_scores, values):
        olds = [m_ref[:, lanes] for lanes, _ in parts]
        news = [
            jnp.maximum(old, jnp.max(scores, axis=0, keepdims=True) * multiplier)
            for old, scores in zip(olds, all_scores)
        ]
        sums = []
        for scores, new in zip(all_scores, news):
            weights = jnp.exp2(scores * multiplier - new).astype(jnp.bfloat16)
            sums.append(jnp.dot(values, weights, preferred_element_type=jnp.float32))
        for (lanes, _), old, new, part in zip(parts, olds, news, sums):
            m_ref[:, lanes] = new
            acc_ref[:, lanes] = acc_ref[:, lanes] * jnp.exp2(old - new) + part

    def score(keys):
        return [
            lax.dot_general(
                keys,
                q_ref[start : start + part_tokens].reshape(LANES, width),
                (((1,), (1,)), ((), ())),
                preferred_element_type=jnp.float32,
            )
            for _, start in parts
        ]

    def one_set(s, carry):
        def one_block(b, inner):
            start = pl.multiple_of(b * KEY_BLOCK, KEY_BLOCK)
            keys = k_ref[s, pl.ds(start, KEY_BLOCK), :]
            values = v_ref[s, :, pl.ds(start, KEY_BLOCK)]
            update(score(keys), values)
            return inner

        return lax.fori_loop(0, counts_ref[s], one_block, carry)

    lax.fori_loop(0, sets, one_set, 0)

    def one_fresh(s, carry):
        all_scores = []
        first = s * fresh_rows
        scores = score(k_ref[s, cache_rows : cache_rows + fresh_rows, :])
        for (lanes, _), part in zip(parts, scores):
            place = first + lax.broadcasted_iota(jnp.int32, part.shape, 0)
            seen = (place >= lo_ref[0:1, lanes]) & (place <= lo_ref[1:2, lanes])
            all_scores.append(jnp.where(seen, part, LOWEST))
        update(all_scores, v_ref[s, :, cache_rows : cache_rows + fresh_rows])
        return carry

    lax.fori_loop(bounds_ref[2 * block], bounds_ref[2 * block + 1], one_fresh, 0)
    for lanes, start in parts:
        total = acc_ref[width : width + 1, lanes]
        out = (acc_ref[0:width, lanes] / total).T
        o_ref[start : start + part_tokens] = out.astype(o_ref.dtype).reshape(
            part_tokens, group, width
        )


def gather_kernel(a_ref, b_ref, a_out, b_out, local_sem, send_sem, recv_sem):
    me = lax.axis_index("ctx")
    column = lax.rem(me // 2, 2)
    line = me // 4
    along_x = me + 2 - 4 * column
    along_y = me + 4 - 8 * line
    across = along_y + 2 - 4 * column
    core = lax.rem(me, 2)
    other = me + 1 - 2 * core

    barrier = pltpu.get_barrier_semaphore()
    for partner in (along_x, along_y, other):
        pl.semaphore_signal(
            barrier, inc=1, device_id={"ctx": partner}, device_id_type=pl.DeviceIdType.MESH
        )
    pl.semaphore_wait(barrier, 3)

    def send(which, slot, source, owner, partner):
        out = (a_out, b_out)[which]
        copy = pltpu.make_async_remote_copy(
            src_ref=source,
            dst_ref=out.at[owner],
            send_sem=send_sem.at[which, slot],
            recv_sem=recv_sem.at[which, slot],
            device_id={"ctx": partner},
            device_id_type=pl.DeviceIdType.MESH,
        )
        copy.start()
        return copy

    copies = []
    keep = []
    for which, (source, out) in enumerate(((a_ref, a_out), (b_ref, b_out))):
        by_x = send(which, 0, source, me, along_x)
        by_y = send(which, 1, source, me, along_y)
        inside = send(which, 2, source, me, other)
        copies.append([by_x, by_y, inside])
        local = pltpu.make_async_copy(source, out.at[me], local_sem.at[which])
        local.start()
        keep.append(local)

    a_copies, b_copies = copies
    a_copies[0].wait_recv()
    a_copies.append(send(0, 3, a_out.at[along_x], along_x, along_y))
    a_copies.append(send(0, 4, a_out.at[along_x], along_x, other))
    b_copies[1].wait_recv()
    b_copies.append(send(1, 3, b_out.at[along_y], along_y, along_x))
    b_copies.append(send(1, 4, b_out.at[along_y], along_y, other))
    a_copies[1].wait_recv()
    a_copies.append(send(0, 5, a_out.at[along_y], along_y, other))
    b_copies[0].wait_recv()
    b_copies.append(send(1, 5, b_out.at[along_x], along_x, other))
    a_copies[3].wait_recv()
    a_copies.append(send(0, 6, a_out.at[across], across, other))
    b_copies[3].wait_recv()
    b_copies.append(send(1, 6, b_out.at[across], across, other))
    for group in copies:
        for slot in (2, 4, 5, 6):
            group[slot].wait_recv()
        for copy in group:
            copy.wait_send()
    for local in keep:
        local.wait()


def gather_pair(a, b, ctx, collective_id):
    if ctx != 8:
        return lax.all_gather(a, "ctx", axis=0), lax.all_gather(b, "ctx", axis=0)
    return pl.pallas_call(
        gather_kernel,
        out_shape=[jax.ShapeDtypeStruct((ctx,) + x.shape, x.dtype) for x in (a, b)],
        in_specs=[pl.BlockSpec(memory_space=pl.ANY)] * 2,
        out_specs=[pl.BlockSpec(memory_space=pl.ANY)] * 2,
        scratch_shapes=[
            pltpu.SemaphoreType.DMA((2,)),
            pltpu.SemaphoreType.DMA((2, 7)),
            pltpu.SemaphoreType.DMA((2, 7)),
        ],
        compiler_params=pltpu.CompilerParams(collective_id=collective_id, has_side_effects=True),
        cost_estimate=pl.CostEstimate(
            flops=0, bytes_accessed=16 * (a.size + b.size), transcendentals=0
        ),
    )(a, b)


def attention(queries, first, tokens, key_sets, value_sets, counts, low, position):
    rows, heads, width = queries.shape
    sets, piece, _ = key_sets.shape
    kv_heads = key_sets.shape[2] // width
    value_rows = value_sets.shape[1] // kv_heads
    group = heads // kv_heads
    cache_rows = piece - rows
    blocks = tokens // TOKEN_BLOCK
    lanes = TOKEN_BLOCK * group
    chunk_low = low[first : first + tokens]
    chunk_position = position[first : first + tokens]
    pair = jnp.stack([chunk_low, chunk_position])
    pair = jnp.repeat(pair, group, axis=1)
    begin = chunk_low[::TOKEN_BLOCK] // rows
    end = chunk_position[TOKEN_BLOCK - 1 :: TOKEN_BLOCK] // rows + 1
    bounds = jnp.stack([begin, end], 1).reshape(-1)
    skip = first // TOKEN_BLOCK
    kernel = functools.partial(
        attention_kernel,
        sets=sets,
        cache_rows=cache_rows,
        fresh_rows=rows,
        multiplier=width**-0.5 * math.log2(math.e),
    )
    total_keys = sets * piece
    return pl.pallas_call(
        kernel,
        out_shape=jax.ShapeDtypeStruct((tokens, heads, width), jnp.bfloat16),
        grid_spec=pltpu.PrefetchScalarGridSpec(
            num_scalar_prefetch=2,
            grid=(kv_heads, blocks),
            in_specs=[
                pl.BlockSpec((TOKEN_BLOCK, group, width), lambda h, i, *_: (i + skip, h, 0)),
                pl.BlockSpec((2, lanes), lambda h, i, *_: (0, i)),
                pl.BlockSpec((sets, piece, width), lambda h, i, *_: (0, 0, h)),
                pl.BlockSpec((sets, value_rows, piece), lambda h, i, *_: (0, h, 0)),
            ],
            out_specs=pl.BlockSpec((TOKEN_BLOCK, group, width), lambda h, i, *_: (i, h, 0)),
            scratch_shapes=[
                pltpu.VMEM((1, lanes), jnp.float32),
                pltpu.VMEM((value_rows, lanes), jnp.float32),
            ],
        ),
        compiler_params=pltpu.CompilerParams(vmem_limit_bytes=48 * 1024 * 1024),
        cost_estimate=pl.CostEstimate(
            flops=4 * tokens * heads * width * total_keys,
            bytes_accessed=4 * total_keys * kv_heads * width,
            transcendentals=tokens * heads * total_keys,
        ),
    )(counts, bounds, queries, pair, key_sets, value_sets)


def pack(keys, fresh_keys, values, fresh_values, length):
    cache_rows, kv_heads, width = keys.shape
    fresh_rows = fresh_keys.shape[0]
    filled = jnp.arange(cache_rows, dtype=jnp.int32) < length
    flat_keys = keys.reshape(cache_rows, kv_heads * width)
    flat_keys = jnp.where(filled[:, None], flat_keys, flat_keys[0:1, :])
    flat_keys = jnp.concatenate([flat_keys, fresh_keys.reshape(fresh_rows, kv_heads * width)], 0)
    flat_values = values.reshape(cache_rows, kv_heads * width)
    flat_values = jnp.where(filled[:, None], flat_values, jnp.zeros_like(flat_values))
    flat_values = jnp.concatenate(
        [flat_values, fresh_values.reshape(fresh_rows, kv_heads * width)], 0
    )
    flat_values = lax.optimization_barrier(flat_values)
    wide = flat_values.T.reshape(kv_heads, width, cache_rows + fresh_rows)
    mask = jnp.concatenate([filled, jnp.ones((fresh_rows,), jnp.bool_)]).astype(jnp.bfloat16)
    mask = jnp.broadcast_to(mask[None, None, :], (kv_heads, 16, cache_rows + fresh_rows))
    wide = jnp.concatenate([wide, mask], 1).reshape(kv_heads * (width + 16), -1)
    return flat_keys, wide


def on_device(
    queries,
    fresh_rotated_keys,
    fresh_value_rows,
    cache_keys,
    prefix_value_rows,
    cache_lengths,
    new_segment,
    out_weight,
    *,
    ctx,
    tp,
):
    rows, heads, width = queries.shape
    kv_heads = fresh_rotated_keys.shape[1]
    cache_rows = cache_keys.shape[0]
    here = lax.axis_index("ctx")
    flat_keys, wide = pack(
        cache_keys, fresh_rotated_keys, prefix_value_rows, fresh_value_rows, cache_lengths[0]
    )
    key_sets, value_sets = gather_pair(flat_keys, wide, ctx, 0)
    lengths = jnp.sum(value_sets[:, width, :cache_rows].astype(jnp.float32), axis=1)
    counts = (lengths.astype(jnp.int32) + KEY_BLOCK - 1) // KEY_BLOCK
    own_segment = lax.dynamic_slice_in_dim(new_segment, here * rows, rows, 0)
    low = jnp.sum((new_segment[None, :] < own_segment[:, None]).astype(jnp.int32), axis=1)
    position = here * rows + jnp.arange(rows, dtype=jnp.int32)

    step = rows // CHUNKS
    attended, mixed = [], []

    def scatter(sums):
        sums = lax.psum_scatter(sums, "tp", scatter_dimension=0, tiled=True)
        return sums.reshape(ctx // tp, -1, sums.shape[-1])

    for c in range(CHUNKS):
        part = attention(
            queries, c * step, step, key_sets, value_sets, counts, low, position
        )
        attended.append(part)
        flat = part.reshape(step, heads * width)
        if c == 0:
            pieces = [lax.all_gather(flat, "ctx", axis=0)]
        else:
            flat, partial = lax.optimization_barrier((flat, partial))
            mixed.append(scatter(partial))
            pieces = gather_pair(flat[: step // 2], flat[step // 2 :], ctx, c)
        for index, piece in enumerate(pieces):
            everyone = piece.reshape(-1, heads * width)
            if index == 1:
                mixed.append(scatter(partial))
                everyone, mixed[-2] = lax.optimization_barrier((everyone, mixed[-2]))
            partial = jnp.dot(everyone, out_weight, preferred_element_type=jnp.float32)
            partial = partial.astype(jnp.bfloat16)
    mixed.append(scatter(partial))
    attended = jnp.concatenate(attended, 0)
    mixed = jnp.concatenate(mixed, 1).reshape(ctx // tp * rows, -1)
    return attended, mixed


def solution(mesh):
    in_specs = (
        P("ctx", "tp", None),
        P("ctx", "tp", None),
        P("ctx", "tp", None),
        P("ctx", "tp", None),
        P("ctx", "tp", None),
        P("ctx"),
        P(),
        P("tp", "ctx"),
    )
    out_specs = (P("ctx", "tp", None), P("tp", "ctx"))
    return jax.shard_map(
        functools.partial(on_device, ctx=mesh.shape["ctx"], tp=mesh.shape["tp"]),
        mesh=mesh,
        in_specs=in_specs,
        out_specs=out_specs,
        check_vma=False,
    )
```
